32 devices in a mesh: domain: 8 (over z, x), band: 4 (over y, core).
Axes of the slice: x: 2, y: 2, z: 4, core: 2. Of those that a mesh axis runs over, the one named last changes fastest.
Arguments:
- orbitals: float32 [96, 48, 16, 128], P('band', 'domain'), may hold values from -8.8 to 8.8
- potential: float32 [48, 16, 128], P('domain', None, 'band'), may hold values from -1.5 to 0
Outputs:
- filtered: float32 [96, 48, 16, 128], P('band', 'domain')
- intersection: float32 [96, 96], P('band')
- hamiltonian: float32 [96, 96], P('band')
The draws below stay inside these ranges and needn't reach their ends.
All inputs are finite; a program needn't handle non-finite values.
Results may differ from the reference program's by a relative error of at most 0.00005.
Values sent between devices are 32-bit elements; how exact they have to be, the bound alone decides.
A program may use at most 64 MiB of HBM per device.

```python
import jax
import jax.numpy as jnp
from jax import lax

ORB = 96
DEGREE = 8
NY = 16
NZ = 128
NX = 48
CELLS = 98304


def draw_orbitals(key, part):
    base = jax.random.fold_in(key, 11)
    key_weight, key_common, key_private = jax.random.split(base, 3)
    weights = jax.random.uniform(key_weight, (ORB, 1, 1, 1), jnp.float32, 0.4, 1.2)
    private = jnp.clip(jax.random.normal(key_private, (ORB, NX, NY, NZ), jnp.float32), -4.0, 4.0)
    common = jnp.clip(jax.random.normal(key_common, (1, NX, NY, NZ), jnp.float32), -4.0, 4.0)
    return private + weights * common


def steps_of(own_key, dims, shards, least, largest):
    gain = 1.0
    for axis_at, parts in shards:
        draws = jax.random.uniform(jax.random.fold_in(jax.random.fold_in(own_key, 6), axis_at), (parts,), jnp.float32, least / len(shards), largest / len(shards))
        gain = gain * jnp.repeat(jnp.exp(draws), dims[axis_at] // parts).reshape((-1,) + (1,) * (len(dims) - 1 - axis_at))
    return gain


def setup_inputs(seed: int = 0) -> dict:
    arg_keys = jax.random.split(jax.random.key(seed), 3)
    return {
        "orbitals": draw_orbitals(jax.random.fold_in(arg_keys[2], 71), 0),
        "potential": jnp.clip(-1.5 + 1.5 * jax.random.uniform(arg_keys[1], (NX, NY, NZ), jnp.float32) ** steps_of(arg_keys[1], (NX, NY, NZ), ((0, 8), (2, 4)), -0.2, 0.2), -1.5, 0.0),
    }


stencil_coeffs = (-5369.0 / 1800.0, 12.0 / 7.0, -15.0 / 56.0, 10.0 / 189.0, -1.0 / 112.0, 2.0 / 1925.0, -1.0 / 16632.0)
stencil_reach = 6
lower_bound = 4.5
upper_bound = 15.5
lowest_bound = 1.0


def laplace(grid_field):
    reach = stencil_reach
    size_y = grid_field.shape[2]
    size_z = grid_field.shape[3]
    padded_yz = jnp.pad(grid_field, ((0, 0), (0, 0), (reach, reach), (reach, reach)))
    summed = (3.0 * stencil_coeffs[0]) * grid_field
    for offset in range(1, reach + 1):
        along_x = jnp.roll(grid_field, -offset, 1) + jnp.roll(grid_field, offset, 1)
        along_y = padded_yz[:, :, reach + offset:reach + offset + size_y, reach:reach + size_z] + padded_yz[:, :, reach - offset:reach - offset + size_y, reach:reach + size_z]
        along_z = padded_yz[:, :, reach:reach + size_y, reach + offset:reach + offset + size_z] + padded_yz[:, :, reach:reach + size_y, reach - offset:reach - offset + size_z]
        summed = summed + stencil_coeffs[offset] * (along_x + along_y + along_z)
    return summed


def apply_hamiltonian(grid_field, potential):
    return -0.5 * laplace(grid_field) + potential[None] * grid_field


def contract(left, right):
    return lax.dot_general(left, right, (((1,), (1,)), ((), ())), precision=lax.Precision.HIGHEST, preferred_element_type=jnp.float32)


def reference(orbitals, potential):
    half_width = (upper_bound - lower_bound) / 2.0
    centre = (upper_bound + lower_bound) / 2.0
    sigma_first = half_width / (lowest_bound - centre)
    previous = orbitals
    current = (apply_hamiltonian(previous, potential) - centre * previous) * (sigma_first / half_width)
    sigma_now = sigma_first
    for degree_step in range(2, DEGREE + 1):
        sigma_next = 1.0 / (2.0 / sigma_first - sigma_now)
        update = (apply_hamiltonian(current, potential) - centre * current) * (2.0 * sigma_next / half_width) - (sigma_now * sigma_next) * previous
        previous = current
        current = update
        sigma_now = sigma_next
    filtered = current
    h_image = apply_hamiltonian(filtered, potential)
    flat_panel = filtered.reshape(ORB, -1)
    flat_image = h_image.reshape(ORB, -1)
    intersection = contract(flat_panel, flat_panel) / CELLS
    hamiltonian = contract(flat_image, flat_panel) / CELLS
    return filtered, intersection, hamiltonian
```

```python
import functools

import jax
import jax.numpy as jnp
from jax import lax
from jax.experimental import pallas as pl
from jax.experimental.pallas import tpu as pltpu
from jax.sharding import PartitionSpec as P
import ml_dtypes
import numpy as np

DEGREE = 8


stencil_coeffs = (
    -5369.0 / 1800.0,
    12.0 / 7.0,
    -15.0 / 56.0,
    10.0 / 189.0,
    -1.0 / 112.0,
    2.0 / 1925.0,
    -1.0 / 16632.0,
)
stencil_reach = 6
lower_bound = 4.5
upper_bound = 15.5
lowest_bound = 1.0


def extended(cells, sides, width):
    for axis, dim in sides:
        count = lax.axis_size(axis)
        head = lax.slice_in_dim(cells, 0, width, axis=dim)
        tail = lax.slice_in_dim(cells, cells.shape[dim] - width, cells.shape[dim], axis=dim)
        cells = jnp.concatenate(
            [
                lax.ppermute(tail, axis, [(i, (i + 1) % count) for i in range(count)]),
                cells,
                lax.ppermute(head, axis, [((i + 1) % count, i) for i in range(count)]),
            ],
            axis=dim,
        )
    return cells


def laplace(grid_field):
    planes = grid_field.shape[1]
    size_y = grid_field.shape[2]
    size_z = grid_field.shape[3]
    padded_x = extended(grid_field, (("domain", 1),), 6)
    padded_yz = jnp.pad(
        grid_field, ((0, 0), (0, 0), (stencil_reach, stencil_reach), (stencil_reach, stencil_reach))
    )
    summed = 3.0 * stencil_coeffs[0] * grid_field
    for offset in range(1, stencil_reach + 1):
        along_x = (
            padded_x[:, stencil_reach + offset : stencil_reach + offset + planes]
            + padded_x[:, stencil_reach - offset : stencil_reach - offset + planes]
        )
        along_y = (
            padded_yz[
                :,
                :,
                stencil_reach + offset : stencil_reach + offset + size_y,
                stencil_reach : stencil_reach + size_z,
            ]
            + padded_yz[
                :,
                :,
                stencil_reach - offset : stencil_reach - offset + size_y,
                stencil_reach : stencil_reach + size_z,
            ]
        )
        along_z = (
            padded_yz[
                :,
                :,
                stencil_reach : stencil_reach + size_y,
                stencil_reach + offset : stencil_reach + offset + size_z,
            ]
            + padded_yz[
                :,
                :,
                stencil_reach : stencil_reach + size_y,
                stencil_reach - offset : stencil_reach - offset + size_z,
            ]
        )
        summed = summed + stencil_coeffs[offset] * (along_x + along_y + along_z)
    return summed


def apply_hamiltonian(grid_field, local_pot):
    return -0.5 * laplace(grid_field) + local_pot[None] * grid_field


def contract(left, right):
    return lax.dot_general(
        left,
        right,
        (((1,), (1,)), ((), ())),
        precision=lax.Precision.HIGHEST,
        preferred_element_type=jnp.float32,
    )


def body_by_block(orbitals, potential):
    local_pot = lax.all_gather(potential, "band", axis=2, tiled=True)
    half_width = (upper_bound - lower_bound) / 2.0
    centre = (upper_bound + lower_bound) / 2.0
    sigma_first = half_width / (lowest_bound - centre)
    previous = orbitals
    current = (apply_hamiltonian(previous, local_pot) - centre * previous) * (
        sigma_first / half_width
    )
    sigma_now = sigma_first
    for degree_step in range(2, DEGREE + 1):
        sigma_next = 1.0 / (2.0 / sigma_first - sigma_now)
        update = (apply_hamiltonian(current, local_pot) - centre * current) * (
            2.0 * sigma_next / half_width
        ) - sigma_now * sigma_next * previous
        previous = current
        current = update
        sigma_now = sigma_next
    h_image = apply_hamiltonian(current, local_pot)
    orb_dev = current.shape[0]
    cell_count = current.shape[1] * current.shape[2] * current.shape[3] * lax.axis_size("domain")
    flat_panel = current.reshape(orb_dev, -1)
    flat_image = h_image.reshape(orb_dev, -1)
    panel_in = lax.all_gather(flat_panel, "band", axis=0, tiled=True)
    s_part = contract(flat_panel, panel_in)
    h_part = contract(flat_image, panel_in)
    s_total, h_total = lax.psum((s_part, h_part), "domain")
    intersection = s_total / cell_count
    hamiltonian = h_total / cell_count
    return (current, intersection, hamiltonian)


pad_rows = 8


def schedule():
    half_width = (upper_bound - lower_bound) / 2.0
    centre = (upper_bound + lower_bound) / 2.0
    sigma_first = half_width / (lowest_bound - centre)
    steps = [(sigma_first / half_width, 0.0)]
    sigma_now = sigma_first
    for degree_step in range(2, DEGREE + 1):
        sigma_next = 1.0 / (2.0 / sigma_first - sigma_now)
        steps.append((2.0 * sigma_next / half_width, sigma_now * sigma_next))
        sigma_now = sigma_next
    return centre, steps


def band_matrix(size):
    full = np.zeros((size, size), np.float64)
    for offset in range(1, stencil_reach + 1):
        full += -0.5 * stencil_coeffs[offset] * (np.eye(size, k=offset) + np.eye(size, k=-offset))
    terms = []
    for _ in range(3):
        terms.append(full.astype(ml_dtypes.bfloat16))
        full = full - terms[-1].astype(np.float64)
    upper = np.concatenate(terms, axis=1)
    lower = np.concatenate([terms[0], terms[1], np.zeros_like(terms[2])], axis=1)
    return np.concatenate([upper, lower], axis=0)


def shifted_h(src, group, groups, shifted_pot, weights):
    reach = stencil_reach
    size_y = src.shape[1] - 2 * pad_rows
    size_z = src.shape[2]
    before = lax.rem(group + groups - 1, groups) * reach
    here = group * reach
    after = lax.rem(group + 1, groups) * reach

    def plane(index, shift=0):
        if index < 0:
            base = before + reach + index
        elif index < reach:
            base = here + index
        else:
            base = after + index - reach
        return src[base, pl.ds(pad_rows + shift, size_y), :]

    center = [plane(i) for i in range(reach)]
    cells = jnp.concatenate(center, axis=0)
    high = cells.astype(jnp.bfloat16)
    low = (cells - high.astype(jnp.float32)).astype(jnp.bfloat16)
    along_z = jnp.dot(
        jnp.concatenate([high, low], axis=1), weights, preferred_element_type=jnp.float32
    )
    along_z = along_z[:, :size_z] + (along_z[:, size_z : 2 * size_z] + along_z[:, 2 * size_z :])
    planes = {i: plane(i) for i in range(-reach, 0)}
    planes.update({i: center[i] for i in range(reach)})
    planes.update({i: plane(i) for i in range(reach, 2 * reach)})
    results = []
    for i in range(reach):
        total = shifted_pot[here + i] * center[i] + along_z[i * size_y : (i + 1) * size_y]
        for offset in range(1, reach + 1):
            pairs = (planes[i + offset] + planes[i - offset]) + (plane(i, offset) + plane(i, -offset))
            total = total + (-0.5 * stencil_coeffs[offset]) * pairs
        results.append(total)
    return results


def filter_kernel(orb_ref, pot_ref, weight_ref, out_ref, image_ref, first, second, shifted_pot):
    count, size_x, size_y, size_z = orb_ref.shape
    reach = stencil_reach
    groups = size_x // reach
    centre, steps = schedule()
    weights = weight_ref[...]
    shifted_pot[...] = pot_ref[...] + (-1.5 * stencil_coeffs[0] - centre)
    zeros = jnp.zeros((size_x, pad_rows, size_z), jnp.float32)
    for buf in (first, second):
        buf[:, pl.ds(0, pad_rows), :] = zeros
        buf[:, pl.ds(pad_rows + size_y, pad_rows), :] = zeros
    inner = pl.ds(pad_rows, size_y)

    def one_orbital(orb, carry):
        first[:, inner, :] = orb_ref[orb]
        buffers = [first, second]
        for scale, back in steps:
            src, dst = buffers

            def one_group(group, carry, src=src, dst=dst, scale=scale, back=back):
                for i, total in enumerate(shifted_h(src, group, groups, shifted_pot, weights)):
                    update = total * scale
                    if back:
                        update = update - back * dst[group * reach + i, inner, :]
                    dst[group * reach + i, inner, :] = update
                return carry

            lax.fori_loop(0, groups, one_group, 0)
            buffers = [dst, src]
        src = buffers[0]

        def image_group(group, carry):
            for i, total in enumerate(shifted_h(src, group, groups, shifted_pot, weights)):
                cells = src[group * reach + i, inner, :]
                out_ref[orb, group * reach + i] = cells
                image_ref[orb, group * reach + i] = total + centre * cells
            return carry

        lax.fori_loop(0, groups, image_group, 0)
        return carry

    lax.fori_loop(0, count, one_orbital, 0)


def filter_orbitals(orbitals, potential):
    count, size_x, size_y, size_z = orbitals.shape
    vmem = pl.BlockSpec(memory_space=pltpu.VMEM)
    padded = pltpu.VMEM((size_x, size_y + 2 * pad_rows, size_z), jnp.float32)
    return pl.pallas_call(
        filter_kernel,
        out_shape=[jax.ShapeDtypeStruct(orbitals.shape, jnp.float32)] * 2,
        in_specs=[vmem] * 3,
        out_specs=[vmem] * 2,
        scratch_shapes=[padded, padded, pltpu.VMEM((size_x, size_y, size_z), jnp.float32)],
        compiler_params=pltpu.CompilerParams(vmem_limit_bytes=32 * 1024 * 1024),
    )(orbitals, potential, jnp.asarray(band_matrix(size_z)))


def greet(peers):
    barrier = pltpu.get_barrier_semaphore()
    for peer in peers:
        pl.semaphore_signal(barrier, inc=1, device_id=peer, device_id_type=pl.DeviceIdType.MESH)
    pl.semaphore_wait(barrier, len(peers))


def others(axis, count):
    me = lax.axis_index(axis)
    return [{axis: lax.rem(me + step, count)} for step in range(1, count)]


def send(src, dst, send_sem, recv_sem, peer):
    copy = pltpu.make_async_remote_copy(
        src_ref=src,
        dst_ref=dst,
        send_sem=send_sem,
        recv_sem=recv_sem,
        device_id=peer,
        device_id_type=pl.DeviceIdType.MESH,
    )
    copy.start()
    return copy


def potential_kernel(domains, bands, part_ref, out_ref, by_band, whole, band_sems, domain_sems):
    planes, size_y, part = part_ref.shape
    band, domain = lax.axis_index("band"), lax.axis_index("domain")
    band_peers, domain_peers = others("band", bands), others("domain", domains)
    greet(band_peers + domain_peers)
    spread = jnp.concatenate([part_ref[...]] * bands, axis=2)
    lane = lax.broadcasted_iota(jnp.int32, spread.shape, 2)
    mine = (lane >= band * part) & (lane < (band + 1) * part)
    by_band[band] = jnp.where(mine, spread, 0.0)
    copies = [
        send(by_band.at[band], by_band.at[band], band_sems.at[0, i], band_sems.at[1, i], peer)
        for i, peer in enumerate(band_peers)
    ]
    for copy in copies:
        copy.wait()
    total = by_band[0]
    for i in range(1, bands):
        total = total + by_band[i]
    block = pl.ds(domain * planes, planes)
    whole[block] = total
    copies = [
        send(whole.at[block], whole.at[block], domain_sems.at[0, i], domain_sems.at[1, i], peer)
        for i, peer in enumerate(domain_peers)
    ]
    for copy in copies:
        copy.wait()
    out_ref[...] = whole[...]


def whole_potential(potential):
    domains, bands = lax.axis_size("domain"), lax.axis_size("band")
    planes, size_y, part = potential.shape
    vmem = pl.BlockSpec(memory_space=pltpu.VMEM)
    whole = (domains * planes, size_y, bands * part)
    return pl.pallas_call(
        functools.partial(potential_kernel, domains, bands),
        out_shape=jax.ShapeDtypeStruct(whole, jnp.float32),
        in_specs=[vmem],
        out_specs=vmem,
        scratch_shapes=[
            pltpu.VMEM((bands, planes, size_y, bands * part), jnp.float32),
            pltpu.VMEM(whole, jnp.float32),
            pltpu.SemaphoreType.DMA((2, bands - 1)),
            pltpu.SemaphoreType.DMA((2, domains - 1)),
        ],
        compiler_params=pltpu.CompilerParams(collective_id=0, has_side_effects=True),
    )(potential)


def tiles_kernel(
    domains, bands, cell_count, field_ref, image_ref, s_ref, h_ref,
    field, image, rows_out, rows_in, part, parts, field_sems, image_sems, own_sems, row_sems, part_sems,
):
    orb_dev, rows, lanes = field_ref.shape
    share = rows // bands
    orbs = orb_dev * bands
    band, domain = lax.axis_index("band"), lax.axis_index("domain")
    band_peers, domain_peers = others("band", bands), others("domain", domains)
    greet(band_peers + domain_peers)
    mine = pl.ds(pl.multiple_of(band * orb_dev, orb_dev), orb_dev)
    copies = []
    for src, dst, sems in ((field_ref, field, field_sems), (image_ref, image, image_sems)):
        for i, peer in enumerate(band_peers):
            cells = pl.ds(pl.multiple_of(peer["band"] * share, share), share)
            copies.append(send(src.at[:, cells], dst.at[mine], sems.at[0, i], sems.at[1, i], peer))
    cells = pl.ds(pl.multiple_of(band * share, share), share)
    for i, (src, dst) in enumerate(((field_ref, field), (image_ref, image))):
        own = pltpu.make_async_copy(src.at[:, cells], dst.at[mine], own_sems.at[i])
        own.start()
        copies.append(own)
    for copy in copies:
        copy.wait()
    total = jnp.zeros((2 * orbs, orbs), jnp.float32)
    for row in range(0, share, 2):
        right = jnp.concatenate([field[:, row, :], field[:, row + 1, :]], axis=1)
        left = jnp.concatenate([image[:, row, :], image[:, row + 1, :]], axis=1)
        total = total + contract(jnp.concatenate([right, left], axis=0), right)
    total = jnp.concatenate([total, jnp.zeros((2 * orbs, lanes - orbs), jnp.float32)], axis=1)
    for peer in range(bands):
        for kind in range(2):
            start = kind * orbs + peer * orb_dev
            rows_out[peer, kind] = total[start : start + orb_dev]
    rows_in[band] = rows_out[band]
    copies = [
        send(rows_out.at[peer["band"]], rows_in.at[band], row_sems.at[0, i], row_sems.at[1, i], peer)
        for i, peer in enumerate(band_peers)
    ]
    for copy in copies:
        copy.wait()
    reduced = rows_in[0]
    for i in range(1, bands):
        reduced = reduced + rows_in[i]
    part[...] = reduced
    parts[domain] = reduced
    copies = [
        send(part, parts.at[domain], part_sems.at[0, i], part_sems.at[1, i], peer)
        for i, peer in enumerate(domain_peers)
    ]
    for copy in copies:
        copy.wait()
    reduced = parts[0]
    for i in range(1, domains):
        reduced = reduced + parts[i]
    reduced = reduced / cell_count
    s_ref[...] = reduced[0, :, :orbs]
    h_ref[...] = reduced[1, :, :orbs]


def tiles(field, image, cell_count):
    domains, bands = lax.axis_size("domain"), lax.axis_size("band")
    orb_dev, rows, lanes = field.shape
    orbs, share = orb_dev * bands, rows // bands
    vmem = pl.BlockSpec(memory_space=pltpu.VMEM)
    pair = (2, orb_dev, lanes)
    gathered = pltpu.VMEM((orbs, share, lanes), jnp.float32)
    return pl.pallas_call(
        functools.partial(tiles_kernel, domains, bands, cell_count),
        out_shape=[jax.ShapeDtypeStruct((orb_dev, orbs), jnp.float32)] * 2,
        in_specs=[vmem] * 2,
        out_specs=[vmem] * 2,
        scratch_shapes=[
            gathered,
            gathered,
            pltpu.VMEM((bands,) + pair, jnp.float32),
            pltpu.VMEM((bands,) + pair, jnp.float32),
            pltpu.VMEM(pair, jnp.float32),
            pltpu.VMEM((domains,) + pair, jnp.float32),
            pltpu.SemaphoreType.DMA((2, bands - 1)),
            pltpu.SemaphoreType.DMA((2, bands - 1)),
            pltpu.SemaphoreType.DMA((2,)),
            pltpu.SemaphoreType.DMA((2, bands - 1)),
            pltpu.SemaphoreType.DMA((2, domains - 1)),
        ],
        compiler_params=pltpu.CompilerParams(
            collective_id=1, has_side_effects=True, vmem_limit_bytes=32 * 1024 * 1024
        ),
    )(field, image)


def body_by_orbital(orbitals, potential):
    orb_dev, planes, size_y, size_z = orbitals.shape
    cell_count = planes * size_y * size_z * lax.axis_size("domain")
    whole = lax.all_to_all(orbitals, "domain", split_axis=0, concat_axis=1, tiled=True)
    filtered, image = filter_orbitals(whole, whole_potential(potential))
    filtered = lax.all_to_all(filtered, "domain", split_axis=1, concat_axis=0, tiled=True)
    image = lax.all_to_all(image, "domain", split_axis=1, concat_axis=0, tiled=True)
    flat = (orb_dev, planes * size_y, size_z)
    intersection, hamiltonian = tiles(filtered.reshape(flat), image.reshape(flat), cell_count)
    return filtered, intersection, hamiltonian


def body(orbitals, potential):
    domains, bands = lax.axis_size("domain"), lax.axis_size("band")
    orb_dev, planes, size_y, size_z = orbitals.shape
    fits = (
        orb_dev % domains == 0
        and orb_dev % 8 == 0
        and planes % stencil_reach == 0
        and size_y % 16 == 0
        and size_z == 128
        and orb_dev * bands <= size_z
        and (planes * size_y) % (8 * bands) == 0
    )
    if fits:
        return body_by_orbital(orbitals, potential)
    return body_by_block(orbitals, potential)


def solution(mesh):
    placed = (P("band", "domain", None, None), P("domain", None, "band"))
    return jax.shard_map(
        body,
        mesh=mesh,
        in_specs=placed,
        out_specs=(P("band", "domain", None, None), P("band", None), P("band", None)),
        check_vma=False,
    )
```

```python
import functools

import jax
import jax.numpy as jnp
from jax import lax
from jax.experimental import pallas as pl
from jax.experimental.pallas import tpu as pltpu
from jax.sharding import PartitionSpec as P
import ml_dtypes
import numpy as np

DEGREE = 8


stencil_coeffs = (
    -5369.0 / 1800.0,
    12.0 / 7.0,
    -15.0 / 56.0,
    10.0 / 189.0,
    -1.0 / 112.0,
    2.0 / 1925.0,
    -1.0 / 16632.0,
)
stencil_reach = 6
lower_bound = 4.5
upper_bound = 15.5
lowest_bound = 1.0


def extended(cells, sides, width):
    for axis, dim in sides:
        count = lax.axis_size(axis)
        head = lax.slice_in_dim(cells, 0, width, axis=dim)
        tail = lax.slice_in_dim(cells, cells.shape[dim] - width, cells.shape[dim], axis=dim)
        cells = jnp.concatenate(
            [
                lax.ppermute(tail, axis, [(i, (i + 1) % count) for i in range(count)]),
                cells,
                lax.ppermute(head, axis, [((i + 1) % count, i) for i in range(count)]),
            ],
            axis=dim,
        )
    return cells


def laplace(grid_field):
    planes = grid_field.shape[1]
    size_y = grid_field.shape[2]
    size_z = grid_field.shape[3]
    padded_x = extended(grid_field, (("domain", 1),), 6)
    padded_yz = jnp.pad(
        grid_field, ((0, 0), (0, 0), (stencil_reach, stencil_reach), (stencil_reach, stencil_reach))
    )
    summed = 3.0 * stencil_coeffs[0] * grid_field
    for offset in range(1, stencil_reach + 1):
        along_x = (
            padded_x[:, stencil_reach + offset : stencil_reach + offset + planes]
            + padded_x[:, stencil_reach - offset : stencil_reach - offset + planes]
        )
        along_y = (
            padded_yz[
                :,
                :,
                stencil_reach + offset : stencil_reach + offset + size_y,
                stencil_reach : stencil_reach + size_z,
            ]
            + padded_yz[
                :,
                :,
                stencil_reach - offset : stencil_reach - offset + size_y,
                stencil_reach : stencil_reach + size_z,
            ]
        )
        along_z = (
            padded_yz[
                :,
                :,
                stencil_reach : stencil_reach + size_y,
                stencil_reach + offset : stencil_reach + offset + size_z,
            ]
            + padded_yz[
                :,
                :,
                stencil_reach : stencil_reach + size_y,
                stencil_reach - offset : stencil_reach - offset + size_z,
            ]
        )
        summed = summed + stencil_coeffs[offset] * (along_x + along_y + along_z)
    return summed


def apply_hamiltonian(grid_field, local_pot):
    return -0.5 * laplace(grid_field) + local_pot[None] * grid_field


def contract(left, right):
    return lax.dot_general(
        left,
        right,
        (((1,), (1,)), ((), ())),
        precision=lax.Precision.HIGHEST,
        preferred_element_type=jnp.float32,
    )


def body_by_block(orbitals, potential):
    local_pot = lax.all_gather(potential, "band", axis=2, tiled=True)
    half_width = (upper_bound - lower_bound) / 2.0
    centre = (upper_bound + lower_bound) / 2.0
    sigma_first = half_width / (lowest_bound - centre)
    previous = orbitals
    current = (apply_hamiltonian(previous, local_pot) - centre * previous) * (
        sigma_first / half_width
    )
    sigma_now = sigma_first
    for degree_step in range(2, DEGREE + 1):
        sigma_next = 1.0 / (2.0 / sigma_first - sigma_now)
        update = (apply_hamiltonian(current, local_pot) - centre * current) * (
            2.0 * sigma_next / half_width
        ) - sigma_now * sigma_next * previous
        previous = current
        current = update
        sigma_now = sigma_next
    h_image = apply_hamiltonian(current, local_pot)
    orb_dev = current.shape[0]
    cell_count = current.shape[1] * current.shape[2] * current.shape[3] * lax.axis_size("domain")
    flat_panel = current.reshape(orb_dev, -1)
    flat_image = h_image.reshape(orb_dev, -1)
    panel_in = lax.all_gather(flat_panel, "band", axis=0, tiled=True)
    s_part = contract(flat_panel, panel_in)
    h_part = contract(flat_image, panel_in)
    s_total, h_total = lax.psum((s_part, h_part), "domain")
    intersection = s_total / cell_count
    hamiltonian = h_total / cell_count
    return (current, intersection, hamiltonian)


pad_rows = 8


def schedule():
    half_width = (upper_bound - lower_bound) / 2.0
    centre = (upper_bound + lower_bound) / 2.0
    sigma_first = half_width / (lowest_bound - centre)
    steps = [(sigma_first / half_width, 0.0)]
    sigma_now = sigma_first
    for degree_step in range(2, DEGREE + 1):
        sigma_next = 1.0 / (2.0 / sigma_first - sigma_now)
        steps.append((2.0 * sigma_next / half_width, sigma_now * sigma_next))
        sigma_now = sigma_next
    return centre, steps


def band_matrix(size):
    full = np.zeros((size, size), np.float64)
    for offset in range(1, stencil_reach + 1):
        full += -0.5 * stencil_coeffs[offset] * (np.eye(size, k=offset) + np.eye(size, k=-offset))
    terms = []
    for _ in range(3):
        terms.append(full.astype(ml_dtypes.bfloat16))
        full = full - terms[-1].astype(np.float64)
    upper = np.concatenate(terms, axis=1)
    lower = np.concatenate([terms[0], terms[1], np.zeros_like(terms[2])], axis=1)
    return np.concatenate([upper, lower], axis=0)


def shifted_h(src, group, groups, shifted_pot, weights):
    reach = stencil_reach
    size_y = src.shape[1] - 2 * pad_rows
    size_z = src.shape[2]
    before = lax.rem(group + groups - 1, groups) * reach
    here = group * reach
    after = lax.rem(group + 1, groups) * reach

    def plane(index, shift=0):
        if index < 0:
            base = before + reach + index
        elif index < reach:
            base = here + index
        else:
            base = after + index - reach
        return src[base, pl.ds(pad_rows + shift, size_y), :]

    center = [plane(i) for i in range(reach)]
    cells = jnp.concatenate(center, axis=0)
    high = cells.astype(jnp.bfloat16)
    low = (cells - high.astype(jnp.float32)).astype(jnp.bfloat16)
    along_z = jnp.dot(
        jnp.concatenate([high, low], axis=1), weights, preferred_element_type=jnp.float32
    )
    along_z = along_z[:, :size_z] + (along_z[:, size_z : 2 * size_z] + along_z[:, 2 * size_z :])
    planes = {i: plane(i) for i in range(-reach, 0)}
    planes.update({i: center[i] for i in range(reach)})
    planes.update({i: plane(i) for i in range(reach, 2 * reach)})
    results = []
    for i in range(reach):
        total = shifted_pot[here + i] * center[i] + along_z[i * size_y : (i + 1) * size_y]
        for offset in range(1, reach + 1):
            pairs = (planes[i + offset] + planes[i - offset]) + (plane(i, offset) + plane(i, -offset))
            total = total + (-0.5 * stencil_coeffs[offset]) * pairs
        results.append(total)
    return results


def greet(peers):
    barrier = pltpu.get_barrier_semaphore()
    for peer in peers:
        pl.semaphore_signal(barrier, inc=1, device_id=peer, device_id_type=pl.DeviceIdType.MESH)
    pl.semaphore_wait(barrier, len(peers))


def others(axis, count):
    me = lax.axis_index(axis)
    return [{axis: lax.rem(me + step, count)} for step in range(1, count)]


def send(src, dst, send_sem, recv_sem, peer):
    copy = pltpu.make_async_remote_copy(
        src_ref=src,
        dst_ref=dst,
        send_sem=send_sem,
        recv_sem=recv_sem,
        device_id=peer,
        device_id_type=pl.DeviceIdType.MESH,
    )
    copy.start()
    return copy


def filter_kernel(
    domains, bands, orb_ref, part_ref, weight_ref, out_ref, image_ref,
    whole_orb, field, image, by_band, whole_pot, first, second,
    band_sems, domain_sems, in_sems, field_sems, image_sems,
):
    count, size_x, size_y, size_z = whole_orb.shape
    planes, _, part = part_ref.shape
    reach = stencil_reach
    groups = size_x // reach
    centre, steps = schedule()
    band, domain = lax.axis_index("band"), lax.axis_index("domain")
    band_peers, domain_peers = others("band", bands), others("domain", domains)
    greet(band_peers + domain_peers)
    block = pl.ds(domain * planes, planes)

    def send_orbital(orb):
        return [
            send(
                orb_ref.at[peer["domain"] * count + orb],
                whole_orb.at[orb, block],
                in_sems.at[0, orb, i],
                in_sems.at[1, orb, i],
                peer,
            )
            for i, peer in enumerate(domain_peers)
        ]

    def send_result(src, dst, sems, orb):
        return [
            send(
                src.at[orb, pl.ds(peer["domain"] * planes, planes)],
                dst.at[domain * count + orb],
                sems.at[0, orb, i],
                sems.at[1, orb, i],
                peer,
            )
            for i, peer in enumerate(domain_peers)
        ]

    spread = jnp.concatenate([part_ref[...]] * bands, axis=2)
    lane = lax.broadcasted_iota(jnp.int32, spread.shape, 2)
    mine = (lane >= band * part) & (lane < (band + 1) * part)
    by_band[band] = jnp.where(mine, spread, 0.0)
    band_copies = [
        send(by_band.at[band], by_band.at[band], band_sems.at[0, i], band_sems.at[1, i], peer)
        for i, peer in enumerate(band_peers)
    ]
    arriving = [send_orbital(0)]
    for copy in band_copies:
        copy.wait()
    total = by_band[0]
    for i in range(1, bands):
        total = total + by_band[i]
    whole_pot[block] = total + (-1.5 * stencil_coeffs[0] - centre)
    pot_copies = [
        send(whole_pot.at[block], whole_pot.at[block], domain_sems.at[0, i], domain_sems.at[1, i], peer)
        for i, peer in enumerate(domain_peers)
    ]
    arriving += [send_orbital(orb) for orb in range(1, count)]
    for orb in range(count):
        whole_orb[orb, block] = orb_ref[domain * count + orb]
    zeros = jnp.zeros((size_x, pad_rows, size_z), jnp.float32)
    for buf in (first, second):
        buf[:, pl.ds(0, pad_rows), :] = zeros
        buf[:, pl.ds(pad_rows + size_y, pad_rows), :] = zeros
    weights = weight_ref[...]
    inner = pl.ds(pad_rows, size_y)
    for copy in pot_copies:
        copy.wait()
    leaving = []
    for orb in range(count):
        for copy in arriving[orb]:
            copy.wait()
        first[:, inner, :] = whole_orb[orb]
        buffers = [first, second]
        for scale, back in steps:
            src, dst = buffers

            def one_group(group, carry, src=src, dst=dst, scale=scale, back=back):
                for i, total in enumerate(shifted_h(src, group, groups, whole_pot, weights)):
                    update = total * scale
                    if back:
                        update = update - back * dst[group * reach + i, inner, :]
                    dst[group * reach + i, inner, :] = update
                return carry

            lax.fori_loop(0, groups, one_group, 0)
            buffers = [dst, src]
        src = buffers[0]
        field[orb] = src[:, inner, :]
        leaving += send_result(field, out_ref, field_sems, orb)

        def image_group(group, carry, src=src, orb=orb):
            for i, total in enumerate(shifted_h(src, group, groups, whole_pot, weights)):
                image[orb, group * reach + i] = total + centre * src[group * reach + i, inner, :]
            return carry

        lax.fori_loop(0, groups, image_group, 0)
        leaving += send_result(image, image_ref, image_sems, orb)
        out_ref[domain * count + orb] = field[orb, block]
        image_ref[domain * count + orb] = image[orb, block]
    for copy in leaving:
        copy.wait()


def filter_orbitals(orbitals, potential):
    domains, bands = lax.axis_size("domain"), lax.axis_size("band")
    orb_dev, planes, size_y, size_z = orbitals.shape
    count, size_x = orb_dev // domains, planes * domains
    vmem = pl.BlockSpec(memory_space=pltpu.VMEM)
    whole = pltpu.VMEM((count, size_x, size_y, size_z), jnp.float32)
    padded = pltpu.VMEM((size_x, size_y + 2 * pad_rows, size_z), jnp.float32)
    by_orbital = pltpu.SemaphoreType.DMA((2, count, domains - 1))
    return pl.pallas_call(
        functools.partial(filter_kernel, domains, bands),
        out_shape=[jax.ShapeDtypeStruct(orbitals.shape, jnp.float32)] * 2,
        in_specs=[vmem] * 3,
        out_specs=[vmem] * 2,
        scratch_shapes=[
            whole,
            whole,
            whole,
            pltpu.VMEM((bands, planes, size_y, size_z), jnp.float32),
            pltpu.VMEM((size_x, size_y, size_z), jnp.float32),
            padded,
            padded,
            pltpu.SemaphoreType.DMA((2, bands - 1)),
            pltpu.SemaphoreType.DMA((2, domains - 1)),
            by_orbital,
            by_orbital,
            by_orbital,
        ],
        compiler_params=pltpu.CompilerParams(
            collective_id=0, has_side_effects=True, vmem_limit_bytes=40 * 1024 * 1024
        ),
    )(orbitals, potential, jnp.asarray(band_matrix(size_z)))


def tiles_kernel(
    domains, bands, cell_count, field_ref, image_ref, s_ref, h_ref,
    field, image, rows_out, rows_in, part, parts, field_sems, image_sems, own_sems, row_sems, part_sems,
):
    orb_dev, rows, lanes = field_ref.shape
    share = rows // bands
    orbs = orb_dev * bands
    band, domain = lax.axis_index("band"), lax.axis_index("domain")
    band_peers, domain_peers = others("band", bands), others("domain", domains)
    greet(band_peers + domain_peers)
    mine = pl.ds(pl.multiple_of(band * orb_dev, orb_dev), orb_dev)
    copies = []
    for src, dst, sems in ((field_ref, field, field_sems), (image_ref, image, image_sems)):
        for i, peer in enumerate(band_peers):
            cells = pl.ds(pl.multiple_of(peer["band"] * share, share), share)
            copies.append(send(src.at[:, cells], dst.at[mine], sems.at[0, i], sems.at[1, i], peer))
    cells = pl.ds(pl.multiple_of(band * share, share), share)
    for i, (src, dst) in enumerate(((field_ref, field), (image_ref, image))):
        own = pltpu.make_async_copy(src.at[:, cells], dst.at[mine], own_sems.at[i])
        own.start()
        copies.append(own)
    for copy in copies:
        copy.wait()
    total = jnp.zeros((2 * orbs, orbs), jnp.float32)
    for row in range(0, share, 2):
        right = jnp.concatenate([field[:, row, :], field[:, row + 1, :]], axis=1)
        left = jnp.concatenate([image[:, row, :], image[:, row + 1, :]], axis=1)
        total = total + contract(jnp.concatenate([right, left], axis=0), right)
    total = jnp.concatenate([total, jnp.zeros((2 * orbs, lanes - orbs), jnp.float32)], axis=1)
    for peer in range(bands):
        for kind in range(2):
            start = kind * orbs + peer * orb_dev
            rows_out[peer, kind] = total[start : start + orb_dev]
    rows_in[band] = rows_out[band]
    copies = [
        send(rows_out.at[peer["band"]], rows_in.at[band], row_sems.at[0, i], row_sems.at[1, i], peer)
        for i, peer in enumerate(band_peers)
    ]
    for copy in copies:
        copy.wait()
    reduced = rows_in[0]
    for i in range(1, bands):
        reduced = reduced + rows_in[i]
    part[...] = reduced
    parts[domain] = reduced
    copies = [
        send(part, parts.at[domain], part_sems.at[0, i], part_sems.at[1, i], peer)
        for i, peer in enumerate(domain_peers)
    ]
    for copy in copies:
        copy.wait()
    reduced = parts[0]
    for i in range(1, domains):
        reduced = reduced + parts[i]
    reduced = reduced / cell_count
    s_ref[...] = reduced[0, :, :orbs]
    h_ref[...] = reduced[1, :, :orbs]


def tiles(field, image, cell_count):
    domains, bands = lax.axis_size("domain"), lax.axis_size("band")
    orb_dev, rows, lanes = field.shape
    orbs, share = orb_dev * bands, rows // bands
    vmem = pl.BlockSpec(memory_space=pltpu.VMEM)
    pair = (2, orb_dev, lanes)
    gathered = pltpu.VMEM((orbs, share, lanes), jnp.float32)
    return pl.pallas_call(
        functools.partial(tiles_kernel, domains, bands, cell_count),
        out_shape=[jax.ShapeDtypeStruct((orb_dev, orbs), jnp.float32)] * 2,
        in_specs=[vmem] * 2,
        out_specs=[vmem] * 2,
        scratch_shapes=[
            gathered,
            gathered,
            pltpu.VMEM((bands,) + pair, jnp.float32),
            pltpu.VMEM((bands,) + pair, jnp.float32),
            pltpu.VMEM(pair, jnp.float32),
            pltpu.VMEM((domains,) + pair, jnp.float32),
            pltpu.SemaphoreType.DMA((2, bands - 1)),
            pltpu.SemaphoreType.DMA((2, bands - 1)),
            pltpu.SemaphoreType.DMA((2,)),
            pltpu.SemaphoreType.DMA((2, bands - 1)),
            pltpu.SemaphoreType.DMA((2, domains - 1)),
        ],
        compiler_params=pltpu.CompilerParams(
            collective_id=1, has_side_effects=True, vmem_limit_bytes=32 * 1024 * 1024
        ),
    )(field, image)


def body_by_orbital(orbitals, potential):
    orb_dev, planes, size_y, size_z = orbitals.shape
    cell_count = planes * size_y * size_z * lax.axis_size("domain")
    filtered, image = filter_orbitals(orbitals, potential)
    flat = (orb_dev, planes * size_y, size_z)
    intersection, hamiltonian = tiles(filtered.reshape(flat), image.reshape(flat), cell_count)
    return filtered, intersection, hamiltonian


def body(orbitals, potential):
    domains, bands = lax.axis_size("domain"), lax.axis_size("band")
    orb_dev, planes, size_y, size_z = orbitals.shape
    fits = (
        orb_dev % domains == 0
        and orb_dev % 8 == 0
        and planes % stencil_reach == 0
        and size_y % 16 == 0
        and size_z == 128
        and orb_dev * bands <= size_z
        and (planes * size_y) % (8 * bands) == 0
    )
    if fits:
        return body_by_orbital(orbitals, potential)
    return body_by_block(orbitals, potential)


def solution(mesh):
    placed = (P("band", "domain", None, None), P("domain", None, "band"))
    return jax.shard_map(
        body,
        mesh=mesh,
        in_specs=placed,
        out_specs=(P("band", "domain", None, None), P("band", None), P("band", None)),
        check_vma=False,
    )
```

```python
import functools

import jax
import jax.numpy as jnp
from jax import lax
from jax.experimental import pallas as pl
from jax.experimental.pallas import tpu as pltpu
from jax.sharding import PartitionSpec as P
import ml_dtypes
import numpy as np

DEGREE = 8


stencil_coeffs = (
    -5369.0 / 1800.0,
    12.0 / 7.0,
    -15.0 / 56.0,
    10.0 / 189.0,
    -1.0 / 112.0,
    2.0 / 1925.0,
    -1.0 / 16632.0,
)
stencil_reach = 6
lower_bound = 4.5
upper_bound = 15.5
lowest_bound = 1.0


def extended(cells, sides, width):
    for axis, dim in sides:
        count = lax.axis_size(axis)
        head = lax.slice_in_dim(cells, 0, width, axis=dim)
        tail = lax.slice_in_dim(cells, cells.shape[dim] - width, cells.shape[dim], axis=dim)
        cells = jnp.concatenate(
            [
                lax.ppermute(tail, axis, [(i, (i + 1) % count) for i in range(count)]),
                cells,
                lax.ppermute(head, axis, [((i + 1) % count, i) for i in range(count)]),
            ],
            axis=dim,
        )
    return cells


def laplace(grid_field):
    planes = grid_field.shape[1]
    size_y = grid_field.shape[2]
    size_z = grid_field.shape[3]
    padded_x = extended(grid_field, (("domain", 1),), 6)
    padded_yz = jnp.pad(
        grid_field, ((0, 0), (0, 0), (stencil_reach, stencil_reach), (stencil_reach, stencil_reach))
    )
    summed = 3.0 * stencil_coeffs[0] * grid_field
    for offset in range(1, stencil_reach + 1):
        along_x = (
            padded_x[:, stencil_reach + offset : stencil_reach + offset + planes]
            + padded_x[:, stencil_reach - offset : stencil_reach - offset + planes]
        )
        along_y = (
            padded_yz[
                :,
                :,
                stencil_reach + offset : stencil_reach + offset + size_y,
                stencil_reach : stencil_reach + size_z,
            ]
            + padded_yz[
                :,
                :,
                stencil_reach - offset : stencil_reach - offset + size_y,
                stencil_reach : stencil_reach + size_z,
            ]
        )
        along_z = (
            padded_yz[
                :,
                :,
                stencil_reach : stencil_reach + size_y,
                stencil_reach + offset : stencil_reach + offset + size_z,
            ]
            + padded_yz[
                :,
                :,
                stencil_reach : stencil_reach + size_y,
                stencil_reach - offset : stencil_reach - offset + size_z,
            ]
        )
        summed = summed + stencil_coeffs[offset] * (along_x + along_y + along_z)
    return summed


def apply_hamiltonian(grid_field, local_pot):
    return -0.5 * laplace(grid_field) + local_pot[None] * grid_field


def contract(left, right):
    return lax.dot_general(
        left,
        right,
        (((1,), (1,)), ((), ())),
        precision=lax.Precision.HIGHEST,
        preferred_element_type=jnp.float32,
    )


def body_by_block(orbitals, potential):
    local_pot = lax.all_gather(potential, "band", axis=2, tiled=True)
    half_width = (upper_bound - lower_bound) / 2.0
    centre = (upper_bound + lower_bound) / 2.0
    sigma_first = half_width / (lowest_bound - centre)
    previous = orbitals
    current = (apply_hamiltonian(previous, local_pot) - centre * previous) * (
        sigma_first / half_width
    )
    sigma_now = sigma_first
    for degree_step in range(2, DEGREE + 1):
        sigma_next = 1.0 / (2.0 / sigma_first - sigma_now)
        update = (apply_hamiltonian(current, local_pot) - centre * current) * (
            2.0 * sigma_next / half_width
        ) - sigma_now * sigma_next * previous
        previous = current
        current = update
        sigma_now = sigma_next
    h_image = apply_hamiltonian(current, local_pot)
    orb_dev = current.shape[0]
    cell_count = current.shape[1] * current.shape[2] * current.shape[3] * lax.axis_size("domain")
    flat_panel = current.reshape(orb_dev, -1)
    flat_image = h_image.reshape(orb_dev, -1)
    panel_in = lax.all_gather(flat_panel, "band", axis=0, tiled=True)
    s_part = contract(flat_panel, panel_in)
    h_part = contract(flat_image, panel_in)
    s_total, h_total = lax.psum((s_part, h_part), "domain")
    intersection = s_total / cell_count
    hamiltonian = h_total / cell_count
    return (current, intersection, hamiltonian)


pad_rows = 8


def schedule():
    half_width = (upper_bound - lower_bound) / 2.0
    centre = (upper_bound + lower_bound) / 2.0
    sigma_first = half_width / (lowest_bound - centre)
    steps = [(sigma_first / half_width, 0.0)]
    sigma_now = sigma_first
    for degree_step in range(2, DEGREE + 1):
        sigma_next = 1.0 / (2.0 / sigma_first - sigma_now)
        steps.append((2.0 * sigma_next / half_width, sigma_now * sigma_next))
        sigma_now = sigma_next
    return centre, steps


def band_matrix(size):
    full = np.zeros((size, size), np.float64)
    for offset in range(1, stencil_reach + 1):
        full += -0.5 * stencil_coeffs[offset] * (np.eye(size, k=offset) + np.eye(size, k=-offset))
    terms = []
    for _ in range(3):
        terms.append(full.astype(ml_dtypes.bfloat16))
        full = full - terms[-1].astype(np.float64)
    upper = np.concatenate(terms, axis=1)
    lower = np.concatenate([terms[0], terms[1], np.zeros_like(terms[2])], axis=1)
    return np.concatenate([upper, lower], axis=0)


def shifted_h(src, group, groups, shifted_pot, weights):
    reach = stencil_reach
    size_y = src.shape[1] - 2 * pad_rows
    size_z = src.shape[2]
    before = lax.rem(group + groups - 1, groups) * reach
    here = group * reach
    after = lax.rem(group + 1, groups) * reach

    def plane(index, shift=0):
        if index < 0:
            base = before + reach + index
        elif index < reach:
            base = here + index
        else:
            base = after + index - reach
        return src[base, pl.ds(pad_rows + shift, size_y), :]

    center = [plane(i) for i in range(reach)]
    cells = jnp.concatenate(center, axis=0)
    high = cells.astype(jnp.bfloat16)
    low = (cells - high.astype(jnp.float32)).astype(jnp.bfloat16)
    along_z = jnp.dot(
        jnp.concatenate([high, low], axis=1), weights, preferred_element_type=jnp.float32
    )
    along_z = along_z[:, :size_z] + (along_z[:, size_z : 2 * size_z] + along_z[:, 2 * size_z :])
    planes = {i: plane(i) for i in range(-reach, 0)}
    planes.update({i: center[i] for i in range(reach)})
    planes.update({i: plane(i) for i in range(reach, 2 * reach)})
    results = []
    for i in range(reach):
        total = shifted_pot[here + i] * center[i] + along_z[i * size_y : (i + 1) * size_y]
        for offset in range(1, reach + 1):
            pairs = (planes[i + offset] + planes[i - offset]) + (plane(i, offset) + plane(i, -offset))
            total = total + (-0.5 * stencil_coeffs[offset]) * pairs
        results.append(total)
    return results


def greet(peers):
    barrier = pltpu.get_barrier_semaphore()
    for peer in peers:
        pl.semaphore_signal(barrier, inc=1, device_id=peer, device_id_type=pl.DeviceIdType.MESH)
    pl.semaphore_wait(barrier, len(peers))


def others(axis, count):
    me = lax.axis_index(axis)
    return [{axis: lax.rem(me + step, count)} for step in range(1, count)]


def send(src, dst, send_sem, recv_sem, peer):
    copy = pltpu.make_async_remote_copy(
        src_ref=src,
        dst_ref=dst,
        send_sem=send_sem,
        recv_sem=recv_sem,
        device_id=peer,
        device_id_type=pl.DeviceIdType.MESH,
    )
    copy.start()
    return copy


def filter_kernel(
    domains, bands, orb_ref, part_ref, weight_ref, out_ref, image_ref,
    whole_orb, field, image, by_band, whole_pot, first, second,
    band_sems, domain_sems, in_sems, field_sems, image_sems,
):
    count, size_x, size_y, size_z = whole_orb.shape
    planes, _, part = part_ref.shape
    reach = stencil_reach
    groups = size_x // reach
    centre, steps = schedule()
    band, domain = lax.axis_index("band"), lax.axis_index("domain")
    band_peers, domain_peers = others("band", bands), others("domain", domains)
    greet(band_peers + domain_peers)
    block = pl.ds(domain * planes, planes)

    def send_orbital(orb):
        return [
            send(
                orb_ref.at[peer["domain"] * count + orb],
                whole_orb.at[orb, block],
                in_sems.at[0, orb, i],
                in_sems.at[1, orb, i],
                peer,
            )
            for i, peer in enumerate(domain_peers)
        ]

    def send_result(src, dst, sems, orb):
        return [
            send(
                src.at[orb, pl.ds(peer["domain"] * planes, planes)],
                dst.at[domain * count + orb],
                sems.at[0, orb, i],
                sems.at[1, orb, i],
                peer,
            )
            for i, peer in enumerate(domain_peers)
        ]

    spread = jnp.concatenate([part_ref[...]] * bands, axis=2)
    lane = lax.broadcasted_iota(jnp.int32, spread.shape, 2)
    mine = (lane >= band * part) & (lane < (band + 1) * part)
    by_band[band] = jnp.where(mine, spread, 0.0)
    band_copies = [
        send(by_band.at[band], by_band.at[band], band_sems.at[0, i], band_sems.at[1, i], peer)
        for i, peer in enumerate(band_peers)
    ]
    arriving = [send_orbital(0)]
    for copy in band_copies:
        copy.wait()
    total = by_band[0]
    for i in range(1, bands):
        total = total + by_band[i]
    whole_pot[block] = total + (-1.5 * stencil_coeffs[0] - centre)
    pot_copies = [
        send(whole_pot.at[block], whole_pot.at[block], domain_sems.at[0, i], domain_sems.at[1, i], peer)
        for i, peer in enumerate(domain_peers)
    ]
    arriving += [send_orbital(orb) for orb in range(1, count)]
    for orb in range(count):
        whole_orb[orb, block] = orb_ref[domain * count + orb]
    zeros = jnp.zeros((size_x, pad_rows, size_z), jnp.float32)
    for buf in (first, second):
        buf[:, pl.ds(0, pad_rows), :] = zeros
        buf[:, pl.ds(pad_rows + size_y, pad_rows), :] = zeros
    weights = weight_ref[...]
    inner = pl.ds(pad_rows, size_y)
    for copy in pot_copies:
        copy.wait()
    leaving = []
    for orb in range(count):
        for copy in arriving[orb]:
            copy.wait()
        first[:, inner, :] = whole_orb[orb]
        buffers = [first, second]
        for scale, back in steps:
            src, dst = buffers

            def one_group(group, carry, src=src, dst=dst, scale=scale, back=back):
                for i, total in enumerate(shifted_h(src, group, groups, whole_pot, weights)):
                    update = total * scale
                    if back:
                        update = update - back * dst[group * reach + i, inner, :]
                    dst[group * reach + i, inner, :] = update
                return carry

            lax.fori_loop(0, groups, one_group, 0)
            buffers = [dst, src]
        src = buffers[0]
        field[orb] = src[:, inner, :]
        leaving += send_result(field, out_ref, field_sems, orb)

        def image_group(group, carry, src=src, orb=orb):
            for i, total in enumerate(shifted_h(src, group, groups, whole_pot, weights)):
                image[orb, group * reach + i] = total + centre * src[group * reach + i, inner, :]
            return carry

        lax.fori_loop(0, groups, image_group, 0)
        leaving += send_result(image, image_ref, image_sems, orb)
        out_ref[domain * count + orb] = field[orb, block]
        image_ref[domain * count + orb] = image[orb, block]
    for copy in leaving:
        copy.wait()


def filter_orbitals(orbitals, potential):
    domains, bands = lax.axis_size("domain"), lax.axis_size("band")
    orb_dev, planes, size_y, size_z = orbitals.shape
    count, size_x = orb_dev // domains, planes * domains
    vmem = pl.BlockSpec(memory_space=pltpu.VMEM)
    whole = pltpu.VMEM((count, size_x, size_y, size_z), jnp.float32)
    padded = pltpu.VMEM((size_x, size_y + 2 * pad_rows, size_z), jnp.float32)
    by_orbital = pltpu.SemaphoreType.DMA((2, count, domains - 1))
    return pl.pallas_call(
        functools.partial(filter_kernel, domains, bands),
        out_shape=[jax.ShapeDtypeStruct(orbitals.shape, jnp.float32)] * 2,
        in_specs=[vmem] * 3,
        out_specs=[vmem] * 2,
        scratch_shapes=[
            whole,
            whole,
            whole,
            pltpu.VMEM((bands, planes, size_y, size_z), jnp.float32),
            pltpu.VMEM((size_x, size_y, size_z), jnp.float32),
            padded,
            padded,
            pltpu.SemaphoreType.DMA((2, bands - 1)),
            pltpu.SemaphoreType.DMA((2, domains - 1)),
            by_orbital,
            by_orbital,
            by_orbital,
        ],
        compiler_params=pltpu.CompilerParams(
            collective_id=0, has_side_effects=True, vmem_limit_bytes=40 * 1024 * 1024
        ),
    )(orbitals, potential, jnp.asarray(band_matrix(size_z)))


def tiles_kernel(
    domains, bands, cell_count, field_ref, image_ref, s_ref, h_ref,
    field, image, rows_out, rows_in, part, parts, field_sems, image_sems, own_sems, row_sems, part_sems,
):
    orb_dev, rows, lanes = field_ref.shape
    share = rows // bands
    orbs = orb_dev * bands
    band, domain = lax.axis_index("band"), lax.axis_index("domain")
    band_peers, domain_peers = others("band", bands), others("domain", domains)
    greet(band_peers + domain_peers)
    mine = pl.ds(pl.multiple_of(band * orb_dev, orb_dev), orb_dev)
    own_cells = pl.ds(pl.multiple_of(band * share, share), share)
    pending = []
    for kind, (src, dst, sems) in enumerate(
        ((field_ref, field, field_sems), (image_ref, image, image_sems))
    ):
        copies = []
        for i, peer in enumerate(band_peers):
            cells = pl.ds(pl.multiple_of(peer["band"] * share, share), share)
            copies.append(send(src.at[:, cells], dst.at[mine], sems.at[0, i], sems.at[1, i], peer))
        own = pltpu.make_async_copy(src.at[:, own_cells], dst.at[mine], own_sems.at[kind])
        own.start()
        pending.append(copies + [own])
    for copy in pending[0]:
        copy.wait()
    rights = []
    s_total = jnp.zeros((orbs, orbs), jnp.float32)
    for row in range(0, share, 2):
        rights.append(jnp.concatenate([field[:, row, :], field[:, row + 1, :]], axis=1))
        s_total = s_total + contract(rights[-1], rights[-1])
    for copy in pending[1]:
        copy.wait()
    h_total = jnp.zeros((orbs, orbs), jnp.float32)
    for row in range(0, share, 2):
        left = jnp.concatenate([image[:, row, :], image[:, row + 1, :]], axis=1)
        h_total = h_total + contract(left, rights[row // 2])
    total = jnp.concatenate([s_total, h_total], axis=0)
    total = jnp.concatenate([total, jnp.zeros((2 * orbs, lanes - orbs), jnp.float32)], axis=1)
    for peer in range(bands):
        for kind in range(2):
            start = kind * orbs + peer * orb_dev
            rows_out[peer, kind] = total[start : start + orb_dev]
    rows_in[band] = rows_out[band]
    copies = [
        send(rows_out.at[peer["band"]], rows_in.at[band], row_sems.at[0, i], row_sems.at[1, i], peer)
        for i, peer in enumerate(band_peers)
    ]
    for copy in copies:
        copy.wait()
    reduced = rows_in[0]
    for i in range(1, bands):
        reduced = reduced + rows_in[i]
    part[...] = reduced
    parts[domain] = reduced
    copies = [
        send(part, parts.at[domain], part_sems.at[0, i], part_sems.at[1, i], peer)
        for i, peer in enumerate(domain_peers)
    ]
    for copy in copies:
        copy.wait()
    reduced = parts[0]
    for i in range(1, domains):
        reduced = reduced + parts[i]
    reduced = reduced / cell_count
    s_ref[...] = reduced[0, :, :orbs]
    h_ref[...] = reduced[1, :, :orbs]


def tiles(field, image, cell_count):
    domains, bands = lax.axis_size("domain"), lax.axis_size("band")
    orb_dev, rows, lanes = field.shape
    orbs, share = orb_dev * bands, rows // bands
    vmem = pl.BlockSpec(memory_space=pltpu.VMEM)
    pair = (2, orb_dev, lanes)
    gathered = pltpu.VMEM((orbs, share, lanes), jnp.float32)
    return pl.pallas_call(
        functools.partial(tiles_kernel, domains, bands, cell_count),
        out_shape=[jax.ShapeDtypeStruct((orb_dev, orbs), jnp.float32)] * 2,
        in_specs=[vmem] * 2,
        out_specs=[vmem] * 2,
        scratch_shapes=[
            gathered,
            gathered,
            pltpu.VMEM((bands,) + pair, jnp.float32),
            pltpu.VMEM((bands,) + pair, jnp.float32),
            pltpu.VMEM(pair, jnp.float32),
            pltpu.VMEM((domains,) + pair, jnp.float32),
            pltpu.SemaphoreType.DMA((2, bands - 1)),
            pltpu.SemaphoreType.DMA((2, bands - 1)),
            pltpu.SemaphoreType.DMA((2,)),
            pltpu.SemaphoreType.DMA((2, bands - 1)),
            pltpu.SemaphoreType.DMA((2, domains - 1)),
        ],
        compiler_params=pltpu.CompilerParams(
            collective_id=1, has_side_effects=True, vmem_limit_bytes=32 * 1024 * 1024
        ),
    )(field, image)


def body_by_orbital(orbitals, potential):
    orb_dev, planes, size_y, size_z = orbitals.shape
    cell_count = planes * size_y * size_z * lax.axis_size("domain")
    filtered, image = filter_orbitals(orbitals, potential)
    flat = (orb_dev, planes * size_y, size_z)
    intersection, hamiltonian = tiles(filtered.reshape(flat), image.reshape(flat), cell_count)
    return filtered, intersection, hamiltonian


def body(orbitals, potential):
    domains, bands = lax.axis_size("domain"), lax.axis_size("band")
    orb_dev, planes, size_y, size_z = orbitals.shape
    fits = (
        orb_dev % domains == 0
        and orb_dev % 8 == 0
        and planes % stencil_reach == 0
        and size_y % 16 == 0
        and size_z == 128
        and orb_dev * bands <= size_z
        and (planes * size_y) % (8 * bands) == 0
    )
    if fits:
        return body_by_orbital(orbitals, potential)
    return body_by_block(orbitals, potential)


def solution(mesh):
    placed = (P("band", "domain", None, None), P("domain", None, "band"))
    return jax.shard_map(
        body,
        mesh=mesh,
        in_specs=placed,
        out_specs=(P("band", "domain", None, None), P("band", None), P("band", None)),
        check_vma=False,
    )
```
